32 devices in a mesh: fibre: 8 (over y, x, core), group: 4 (over z).
Axes of the slice: x: 2, y: 2, z: 4, core: 2. Of those that a mesh axis runs over, the one named last changes fastest.
Arguments:
- tensor: float32 [512, 49152], P('fibre', 'group'), as said below
Outputs:
- basis: float32 [512, 49152], P('fibre', 'group')
- factor: float32 [512, 512], replicated
Inputs may be any that keep to these rules, and one draw needn't show every extreme that they name: `tensor`: entries are real-valued and the unfolding has full row rank.
All inputs are finite; a program needn't handle non-finite values.
Results may differ from the reference program's by a relative error of at most 0.00018.
Values sent between devices are 32-bit elements; how exact they have to be, the bound alone decides.
No kernel may reach another device: no remote copies, remote signals or barrier semaphores. Data moves between devices by JAX's collectives and lax.ppermute only.
A program may use at most 64 MiB of HBM per device.

```python
import jax
import jax.numpy as jnp
from jax import lax

M = 512
ROWS_DEV = 1536
COLS = 49152
N_FIBRE = 8
N_GROUP = 4


def draw_tensor(key, part):
    keys = jax.random.split(key, 6)
    base = jax.random.normal(keys[0], (M, COLS), jnp.float32)
    loadings = jax.random.normal(keys[4], (M, 8), jnp.float32) / jnp.sqrt(8.0)
    common = jax.random.normal(keys[5], (8, COLS), jnp.float32)
    shared = jnp.zeros((M, COLS), jnp.float32)
    for factor_index in range(8):
        shared = shared + loadings[:, factor_index:factor_index + 1] * common[factor_index:factor_index + 1, :]
    base = base + 0.8 * shared
    row_scale = jnp.exp(jax.random.uniform(keys[1], (M, 1), jnp.float32) * jnp.log(4.0))
    position = jnp.arange(COLS, dtype=jnp.float32).reshape(1, COLS) / COLS
    col_scale = jnp.exp(position * jnp.log(3.0) + jax.random.uniform(keys[2], (1, COLS), jnp.float32, -0.3, 0.3))
    return (base * row_scale * col_scale).astype(jnp.float32)


def setup_inputs(seed: int = 0) -> dict:
    splits = jax.random.split(jax.random.key(seed), 2)
    return {
        "tensor": draw_tensor(jax.random.fold_in(splits[1], 71), 0),
    }


def reference(tensor):
    count_f = N_FIBRE
    count_g = N_GROUP
    total_cols = ROWS_DEV * count_f * count_g
    blocks = tensor.reshape(M, count_g, count_f, ROWS_DEV).transpose(2, 1, 0, 3).reshape(count_f * count_g, M, ROWS_DEV)

    def add_gram(carry, block):
        gram = jnp.dot(block.astype(jnp.float32), block.T.astype(jnp.float32), precision=lax.Precision.HIGHEST, preferred_element_type=jnp.float32) / total_cols
        return (carry + gram, None)
    total, unused = lax.scan(add_gram, jnp.zeros((M, M), jnp.float32), blocks)
    factor = jnp.linalg.cholesky(total)

    def solve_block(block):
        return lax.linalg.triangular_solve(factor, block, left_side=True, lower=True)
    solved = lax.map(solve_block, blocks).reshape(count_f, count_g, M, ROWS_DEV)
    basis = solved.transpose(2, 1, 0, 3).reshape(M, total_cols)
    return (basis, factor)
```

```python
import functools

import jax
import jax.numpy as jnp
from jax import lax
from jax.experimental import pallas as pl
from jax.experimental.pallas import tpu as pltpu
from jax.sharding import PartitionSpec as P

LANES = 128
SUB = 8
PART = 32
MIB = 1024 * 1024


def split(x):
    high = x.astype(jnp.bfloat16)
    return high, (x - high.astype(jnp.float32)).astype(jnp.bfloat16)


def dot3(a, b, dims):
    (ah, al), (bh, bl) = a, b
    one = functools.partial(
        lax.dot_general, dimension_numbers=(dims, ((), ())), preferred_element_type=jnp.float32
    )
    return one(ah, bh) + (one(ah, bl) + one(al, bh))


def dot_full(a, b, dims):
    return lax.dot_general(
        a, b, (dims, ((), ())), precision=lax.Precision.HIGHEST, preferred_element_type=jnp.float32
    )


def packed_blocks(m):
    return [
        (r, c)
        for r in range(0, m, PART)
        for c in range(0, r + PART, LANES)
    ]


def gram_kernel(scale, x_ref, out_ref, high, low):
    m = x_ref.shape[0]
    half = m // 2
    high[...], low[...] = split(x_ref[...])
    blocks = packed_blocks(m)
    for start in (0, half):
        rows, upto = slice(start, start + half), slice(0, start + half)
        g = dot3((high[rows, :], low[rows, :]), (high[upto, :], low[upto, :]), ((1,), (1,))) * scale
        for i, (r, c) in enumerate(blocks):
            if start <= r < start + half:
                out_ref[i * PART : (i + 1) * PART, :] = g[r - start : r - start + PART, c : c + LANES]


def gram_packed(x, scale):
    m, n = x.shape
    return pl.pallas_call(
        functools.partial(gram_kernel, scale),
        out_shape=jax.ShapeDtypeStruct((len(packed_blocks(m)) * PART, LANES), jnp.float32),
        scratch_shapes=[pltpu.VMEM((m, n), jnp.bfloat16)] * 2,
        compiler_params=pltpu.CompilerParams(vmem_limit_bytes=32 * MIB),
        cost_estimate=pl.CostEstimate(
            flops=6 * m * m * n * 3 // 4, bytes_accessed=4 * m * n, transcendentals=0
        ),
        name="gram",
    )(x)


def along_lanes(v, j):
    return jnp.broadcast_to(v[:, j : j + 1], (SUB, LANES))


def along_sublanes(v, s):
    return jnp.broadcast_to(v[s : s + 1, :], (SUB, LANES))


def factor_block(x, z):
    sub = lax.broadcasted_iota(jnp.int32, (SUB, LANES), 0)
    for g in range(len(x)):
        cols = [along_lanes(x[g], SUB * g + t) for t in range(SUB)]
        x_rows, z_rows, inverses, r = [], [], [], {}
        xg, zg = x[g], z[g]
        for t in range(SUB):
            inverse = lax.rsqrt(along_sublanes(cols[t], t))
            m = jnp.where(sub > t, cols[t] * inverse, 0.0)
            x_row, z_row = along_sublanes(xg, t) * inverse, along_sublanes(zg, t) * inverse
            xg = jnp.where(sub == t, x_row, xg - m * x_row)
            zg = jnp.where(sub == t, z_row, zg - m * z_row)
            for u in range(t + 1, SUB):
                r[t, u] = along_sublanes(cols[u], t) * inverse
                cols[u] = cols[u] - m * r[t, u]
            x_rows.append(x_row)
            z_rows.append(z_row)
            inverses.append(inverse)
        x[g], z[g] = xg, zg
        for h in range(g + 1, len(x)):
            cols = [along_lanes(x[h], SUB * g + t) for t in range(SUB)]
            for t in range(SUB):
                cols[t] = cols[t] * inverses[t]
                for u in range(t + 1, SUB):
                    cols[u] = cols[u] - cols[t] * r[t, u]
                x[h] = x[h] - cols[t] * x_rows[t]
                z[h] = z[h] - cols[t] * z_rows[t]
    return jnp.concatenate(x, 0), jnp.concatenate(z, 0)


def factor_kernel(m, g_ref, l_ref, w_ref, a_ref):
    for i, (r, c) in enumerate(packed_blocks(m)):
        a_ref[r : r + PART, c : c + LANES] = g_ref[i * PART : (i + 1) * PART, :]
    l_ref[...] = jnp.zeros((m, m), jnp.float32)
    w_ref[...] = jnp.zeros((m, m), jnp.float32)
    row = lax.broadcasted_iota(jnp.int32, (LANES, LANES), 0)
    lane = lax.broadcasted_iota(jnp.int32, (LANES, LANES), 1)
    groups = range(0, LANES, SUB)
    for k in range(0, m, LANES):
        ks = slice(k, k + LANES)
        x = [a_ref[k + s : k + s + SUB, ks] for s in groups]
        z = [(lane[s : s + SUB] == row[s : s + SUB]).astype(jnp.float32) for s in groups]
        upper, inverse = factor_block(x, z)
        l_ref[ks, ks] = jnp.where(row >= lane, upper.T, 0.0)
        w_ref[ks, ks] = inverse
        if k + LANES < m:
            rest = slice(k + LANES, m)
            panel = dot_full(a_ref[rest, ks], inverse, ((1,), (1,)))
            l_ref[rest, ks] = panel
            a_ref[rest, rest] = a_ref[rest, rest] - dot_full(panel, panel, ((1,), (1,)))
    for i in range(LANES, m, LANES):
        rows = slice(i, i + LANES)
        acc = dot_full(l_ref[rows, 0:i], w_ref[0:i, 0:i], ((1,), (0,)))
        w_ref[rows, 0:i] = -dot_full(w_ref[rows, rows], acc, ((1,), (0,)))


def factor_and_inverse(packed, m):
    return pl.pallas_call(
        functools.partial(factor_kernel, m),
        out_shape=[jax.ShapeDtypeStruct((m, m), jnp.float32)] * 2,
        scratch_shapes=[pltpu.VMEM((m, m), jnp.float32)],
        compiler_params=pltpu.CompilerParams(vmem_limit_bytes=32 * MIB),
        cost_estimate=pl.CostEstimate(flops=12 * m * m * m, bytes_accessed=12 * m * m, transcendentals=m),
        name="factor",
    )(packed)


def apply_kernel(w_ref, x_ref, out_ref):
    m = w_ref.shape[0]
    half = m // 2
    x = split(x_ref[...])
    w = split(w_ref[...])
    for start in (0, half):
        rows, upto = slice(start, start + half), slice(0, start + half)
        out_ref[rows, :] = dot3([v[rows, upto] for v in w], [v[upto, :] for v in x], ((1,), (0,)))


def apply_inverse(w, x):
    m, n = x.shape
    tile = n // 3
    return pl.pallas_call(
        apply_kernel,
        grid=(n // tile,),
        in_specs=[
            pl.BlockSpec((m, m), lambda i: (0, 0)),
            pl.BlockSpec((m, tile), lambda i: (0, i)),
        ],
        out_specs=pl.BlockSpec((m, tile), lambda i: (0, i)),
        out_shape=jax.ShapeDtypeStruct((m, n), jnp.float32),
        compiler_params=pltpu.CompilerParams(vmem_limit_bytes=32 * MIB),
        cost_estimate=pl.CostEstimate(
            flops=6 * m * m * n * 3 // 4, bytes_accessed=8 * m * n, transcendentals=0
        ),
        name="apply",
    )(w, x)


def permute(x, axis, bits):
    return lax.ppermute(x, axis, [(i, i ^ bits) for i in range(lax.axis_size(axis))])


def tree_sum(terms):
    while len(terms) > 1:
        terms = [a + b for a, b in zip(terms[::2], terms[1::2], strict=True)]
    return terms[0]


def sum_everywhere(packed):
    chips = lax.axis_size("fibre") // 2
    me = lax.axis_index("fibre")
    core, chip = lax.rem(me, 2), lax.div(me, 2)
    pieces = packed.reshape(2, chips, -1, LANES)
    mine = lax.dynamic_index_in_dim(pieces, core, 0, keepdims=False)
    theirs = lax.dynamic_index_in_dim(pieces, 1 - core, 0, keepdims=False)
    mine = mine + permute(theirs, "fibre", 1)
    piece = tree_sum(
        [
            lax.dynamic_index_in_dim(mine, chip, 0, keepdims=False)
            if k == 0
            else permute(lax.dynamic_index_in_dim(mine, chip ^ k, 0, keepdims=False), "fibre", 2 * k)
            for k in range(chips)
        ]
    )
    piece = tree_sum(
        [piece if k == 0 else permute(piece, "group", k) for k in range(lax.axis_size("group"))]
    )
    gathered = jnp.zeros((chips, *piece.shape), piece.dtype)
    for k in range(chips):
        part = piece if k == 0 else permute(piece, "fibre", 2 * k)
        gathered = lax.dynamic_update_index_in_dim(gathered, part, chip ^ k, 0)
    other = permute(gathered, "fibre", 1)
    low = jnp.where(core == 0, gathered, other)
    high = jnp.where(core == 0, other, gathered)
    return jnp.stack([low, high]).reshape(packed.shape)


def local(tensor):
    columns = lax.all_to_all(tensor, "fibre", split_axis=1, concat_axis=0, tiled=True)
    m, n = columns.shape
    total_cols = n * lax.axis_size("fibre") * lax.axis_size("group")
    total = sum_everywhere(gram_packed(columns, 1.0 / total_cols))
    factor, inverse = factor_and_inverse(total, m)
    solved = apply_inverse(inverse, columns)
    basis = lax.all_to_all(solved, "fibre", split_axis=0, concat_axis=1, tiled=True)
    return (basis, factor)


def solution(mesh):
    return jax.shard_map(
        local,
        mesh=mesh,
        in_specs=(P("fibre", "group"),),
        out_specs=(P("fibre", "group"), P()),
        check_vma=False,
    )
```

```python
import functools

import jax
import jax.numpy as jnp
from jax import lax
from jax.experimental import pallas as pl
from jax.experimental.pallas import tpu as pltpu
from jax.sharding import PartitionSpec as P

LANES = 128
SUB = 8
PART = 32
MIB = 1024 * 1024


def split(x):
    high = x.astype(jnp.bfloat16)
    return high, (x - high.astype(jnp.float32)).astype(jnp.bfloat16)


def dot3(a, b, dims):
    (ah, al), (bh, bl) = a, b
    one = functools.partial(
        lax.dot_general, dimension_numbers=(dims, ((), ())), preferred_element_type=jnp.float32
    )
    return one(ah, bh) + (one(ah, bl) + one(al, bh))


def dot_full(a, b, dims):
    return lax.dot_general(
        a, b, (dims, ((), ())), precision=lax.Precision.HIGHEST, preferred_element_type=jnp.float32
    )


def packed_blocks(m):
    return [
        (r, c)
        for r in range(0, m, PART)
        for c in range(0, r + PART, LANES)
    ]


def fibre_index():
    return lax.axis_index("fibre")


def place_rows(parts, high, low):
    rows = parts[0].shape[0]
    me = fibre_index()
    for k, part in enumerate(parts):
        at = pl.ds(pl.multiple_of((me ^ k) * rows, rows), rows)
        high[at, :], low[at, :] = split(part[...])


def gram_kernel(scale, n, *refs):
    parts, (mine, theirs, high, low, packed) = refs[:n], refs[n:]
    m = high.shape[0]
    half = m // 2
    place_rows(parts, high, low)
    blocks = packed_blocks(m)
    for start in (0, half):
        rows, upto = slice(start, start + half), slice(0, start + half)
        g = dot3((high[rows, :], low[rows, :]), (high[upto, :], low[upto, :]), ((1,), (1,))) * scale
        for i, (r, c) in enumerate(blocks):
            if start <= r < start + half:
                packed[i * PART : (i + 1) * PART, :] = g[r - start : r - start + PART, c : c + LANES]
    me = fibre_index()
    piece = packed.shape[0] // n
    for k in range(0, n, 2):
        to = slice(k // 2 * piece, (k // 2 + 1) * piece)
        mine[to, :] = packed[pl.ds(pl.multiple_of(piece_of(me ^ k, n) * piece, SUB), piece), :]
        theirs[to, :] = packed[pl.ds(pl.multiple_of(piece_of(me ^ k ^ 1, n) * piece, SUB), piece), :]


def piece_of(device, n):
    return device


def gram_packed(parts, scale):
    rows, w = parts[0].shape
    n = len(parts)
    m = rows * n
    size = len(packed_blocks(m)) * PART
    half = jax.ShapeDtypeStruct((size // 2, LANES), jnp.float32)
    wide = jax.ShapeDtypeStruct((m, w), jnp.bfloat16)
    return pl.pallas_call(
        functools.partial(gram_kernel, scale, n),
        out_shape=[half, half, wide, wide],
        scratch_shapes=[pltpu.VMEM((size, LANES), jnp.float32)],
        compiler_params=pltpu.CompilerParams(vmem_limit_bytes=24 * MIB),
        cost_estimate=pl.CostEstimate(
            flops=6 * m * m * w * 3 // 4, bytes_accessed=4 * m * w, transcendentals=0
        ),
        name="gram",
    )(*parts)


def along_lanes(v, j):
    return jnp.broadcast_to(v[:, j : j + 1], (SUB, LANES))


def along_sublanes(v, s):
    return jnp.broadcast_to(v[s : s + 1, :], (SUB, LANES))


def factor_block(x, z):
    sub = lax.broadcasted_iota(jnp.int32, (SUB, LANES), 0)
    for g in range(len(x)):
        cols = [along_lanes(x[g], SUB * g + t) for t in range(SUB)]
        x_rows, z_rows, inverses, r = [], [], [], {}
        xg, zg = x[g], z[g]
        for t in range(SUB):
            inverse = lax.rsqrt(along_sublanes(cols[t], t))
            m = jnp.where(sub > t, cols[t] * inverse, 0.0)
            x_row, z_row = along_sublanes(xg, t) * inverse, along_sublanes(zg, t) * inverse
            xg = jnp.where(sub == t, x_row, xg - m * x_row)
            zg = jnp.where(sub == t, z_row, zg - m * z_row)
            for u in range(t + 1, SUB):
                r[t, u] = along_sublanes(cols[u], t) * inverse
                cols[u] = cols[u] - m * r[t, u]
            x_rows.append(x_row)
            z_rows.append(z_row)
            inverses.append(inverse)
        x[g], z[g] = xg, zg
        for h in range(g + 1, len(x)):
            cols = [along_lanes(x[h], SUB * g + t) for t in range(SUB)]
            for t in range(SUB):
                cols[t] = cols[t] * inverses[t]
                for u in range(t + 1, SUB):
                    cols[u] = cols[u] - cols[t] * r[t, u]
                x[h] = x[h] - cols[t] * x_rows[t]
                z[h] = z[h] - cols[t] * z_rows[t]
    return jnp.concatenate(x, 0), jnp.concatenate(z, 0)


def factor_kernel(m, n, *refs):
    pieces, (l_ref, w_ref, a_ref, packed) = refs[:n], refs[n:]
    piece = pieces[0].shape[0]
    me = fibre_index()
    for k, part in enumerate(pieces):
        packed[pl.ds(pl.multiple_of(piece_of(me ^ k, n) * piece, SUB), piece), :] = part[...]
    for i, (r, c) in enumerate(packed_blocks(m)):
        a_ref[r : r + PART, c : c + LANES] = packed[i * PART : (i + 1) * PART, :]
    l_ref[...] = jnp.zeros((m, m), jnp.float32)
    w_ref[...] = jnp.zeros((m, m), jnp.float32)
    row = lax.broadcasted_iota(jnp.int32, (LANES, LANES), 0)
    lane = lax.broadcasted_iota(jnp.int32, (LANES, LANES), 1)
    groups = range(0, LANES, SUB)
    for k in range(0, m, LANES):
        ks = slice(k, k + LANES)
        x = [a_ref[k + s : k + s + SUB, ks] for s in groups]
        z = [(lane[s : s + SUB] == row[s : s + SUB]).astype(jnp.float32) for s in groups]
        upper, inverse = factor_block(x, z)
        l_ref[ks, ks] = jnp.where(row >= lane, upper.T, 0.0)
        w_ref[ks, ks] = inverse
        if k + LANES < m:
            rest = slice(k + LANES, m)
            panel = dot_full(a_ref[rest, ks], inverse, ((1,), (1,)))
            l_ref[rest, ks] = panel
            a_ref[rest, rest] = a_ref[rest, rest] - dot_full(panel, panel, ((1,), (1,)))
    for i in range(LANES, m, LANES):
        rows = slice(i, i + LANES)
        acc = dot_full(l_ref[rows, 0:i], w_ref[0:i, 0:i], ((1,), (0,)))
        w_ref[rows, 0:i] = -dot_full(w_ref[rows, rows], acc, ((1,), (0,)))


def factor_and_inverse(pieces, m):
    n = len(pieces)
    return pl.pallas_call(
        functools.partial(factor_kernel, m, n),
        out_shape=[jax.ShapeDtypeStruct((m, m), jnp.float32)] * 2,
        scratch_shapes=[
            pltpu.VMEM((m, m), jnp.float32),
            pltpu.VMEM((n * pieces[0].shape[0], LANES), jnp.float32),
        ],
        compiler_params=pltpu.CompilerParams(vmem_limit_bytes=24 * MIB),
        cost_estimate=pl.CostEstimate(
            flops=160 * m * m * m, bytes_accessed=12 * m * m, transcendentals=m
        ),
        name="factor",
    )(*pieces)


def rows_of(w_ref, wide, ks, rows):
    me = fibre_index()
    for i, k in enumerate(ks):
        piece = w_ref[pl.ds(pl.multiple_of((me ^ k) * rows, rows), rows), :]
        high, low = split(piece)
        for half, value in zip(wide, (high, low), strict=True):
            half[i * rows : (i + 1) * rows, :] = value


def send_kernel(ks, w_ref, high, low, *refs):
    outs, wide = refs[: len(ks)], refs[len(ks) :]
    rows, width = outs[0].shape
    rows_of(w_ref, wide, ks, rows)
    for start in range(0, width, width // 2):
        cols = slice(start, start + width // 2)
        solved = dot3((wide[0][...], wide[1][...]), (high[:, cols], low[:, cols]), ((1,), (0,)))
        for i, out in enumerate(outs):
            out[:, cols] = solved[i * rows : (i + 1) * rows]


def rows_to_send(w, high, low, ks, rows):
    m, width = high.shape
    return pl.pallas_call(
        functools.partial(send_kernel, ks),
        out_shape=[jax.ShapeDtypeStruct((rows, width), jnp.float32)] * len(ks),
        scratch_shapes=[pltpu.VMEM((len(ks) * rows, m), jnp.bfloat16)] * 2,
        compiler_params=pltpu.CompilerParams(vmem_limit_bytes=24 * MIB),
        cost_estimate=pl.CostEstimate(
            flops=6 * len(ks) * rows * m * width, bytes_accessed=8 * m * width, transcendentals=0
        ),
        name="send_rows",
    )(w, high, low)


def keep_kernel(n, w_ref, high, low, *refs):
    parts, outs, (twin_high, twin_low), wide = refs[:n], refs[n : n + 4], refs[n + 4 : n + 6], refs[n + 6 :]
    rows, width = outs[0].shape
    rows_of(w_ref, wide, (0, 1), rows)
    place_rows(parts, twin_high, twin_low)
    for first, (h, l) in ((0, (high, low)), (2, (twin_high, twin_low))):
        for start in range(0, width, width // 2):
            cols = slice(start, start + width // 2)
            solved = dot3((wide[0][...], wide[1][...]), (h[:, cols], l[:, cols]), ((1,), (0,)))
            outs[first][:, cols] = solved[:rows]
            outs[first + 1][:, cols] = solved[rows:]


def rows_to_keep(w, high, low, twin):
    m, width = high.shape
    n = len(twin)
    rows = m // n
    return pl.pallas_call(
        functools.partial(keep_kernel, n),
        out_shape=[jax.ShapeDtypeStruct((rows, width), jnp.float32)] * 4,
        scratch_shapes=[pltpu.VMEM((m, width), jnp.bfloat16)] * 2 + [pltpu.VMEM((2 * rows, m), jnp.bfloat16)] * 2,
        compiler_params=pltpu.CompilerParams(vmem_limit_bytes=24 * MIB),
        cost_estimate=pl.CostEstimate(
            flops=24 * rows * m * width, bytes_accessed=8 * m * width, transcendentals=0
        ),
        name="keep_rows",
    )(w, high, low, *twin)


def permute(x, axis, bits):
    return lax.ppermute(x, axis, [(i, i ^ bits) for i in range(lax.axis_size(axis))])


def tree_sum(terms):
    while len(terms) > 1:
        terms = [a + b for a, b in zip(terms[::2], terms[1::2], strict=True)]
    return terms[0]


def after(x, *earlier):
    return lax.optimization_barrier((x, *earlier))[0]


def local(tensor):
    n = lax.axis_size("fibre")
    groups = lax.axis_size("group")
    chips = n // 2
    me = lax.axis_index("fibre")
    rows, wide = tensor.shape
    m, width = rows * n, wide // n
    opposite = n - 2

    def block(x, j):
        return lax.dynamic_slice(x, (0, j * width), (rows, width))

    far_first = sorted(range(1, n), key=lambda k: -k)
    parts = [block(tensor, me)] + [None] * (n - 1)
    for k in far_first:
        parts[k] = permute(block(tensor, me ^ k), "fibre", k)
    twin = [block(tensor, me ^ opposite)] + [None] * (n - 1)

    def send_twin(ks, *earlier):
        for k in ks:
            x = block(tensor, me ^ k ^ opposite)
            twin[k] = permute(after(x, *earlier) if earlier else x, "fibre", k)

    odd = [k for k in range(3, n - 2, 2)]
    even = [k for k in range(2, n - 2, 2)]
    send_twin(odd)
    mine, theirs, high, low = gram_packed(parts, 1.0 / (width * n * groups))
    mine = (mine + permute(theirs, "fibre", 1)).reshape(chips, -1, LANES)
    piece = tree_sum([mine[k] if k == 0 else permute(mine[k], "fibre", 2 * k) for k in range(chips)])
    send_twin(even, piece)
    piece = tree_sum([piece if k == 0 else permute(piece, "group", k) for k in range(groups)])
    pieces = [None] * n
    for k in range(chips):
        pieces[2 * k] = piece if k == 0 else permute(piece, "fibre", 2 * k)
        pieces[2 * k + 1] = permute(pieces[2 * k], "fibre", 1)
    send_twin((n - 1, n - 2, 1), pieces[2])
    factor, inverse = factor_and_inverse(pieces, m)
    ks = tuple(range(2, n - 2))
    solved = rows_to_send(inverse, high, low, ks, rows)
    out = {k: permute(x, "fibre", k) for k, x in zip(ks, solved, strict=True)}
    out[0], near, out[opposite], twin_near = rows_to_keep(inverse, high, low, twin)
    out[1] = permute(near, "fibre", 1)
    out[opposite + 1] = permute(twin_near, "fibre", 1)
    basis = jnp.zeros((rows, wide), jnp.float32)
    for k in (0, opposite, 1, opposite + 1, *ks):
        basis = lax.dynamic_update_slice(basis, out[k], (0, (me ^ k) * width))
    return (basis, factor)


def solution(mesh):
    return jax.shard_map(
        local,
        mesh=mesh,
        in_specs=(P("fibre", "group"),),
        out_specs=(P("fibre", "group"), P()),
        check_vma=False,
    )
```

```python
import functools

import jax
import jax.numpy as jnp
from jax import lax
from jax.experimental import pallas as pl
from jax.experimental.pallas import tpu as pltpu
from jax.sharding import PartitionSpec as P

LANES = 128
SUB = 8
PART = 32
MIB = 1024 * 1024
SHORT = pl.CostEstimate(flops=1024, bytes_accessed=1024, transcendentals=0)
KEEP = SHORT


def split(x):
    high = x.astype(jnp.bfloat16)
    return high, (x - high.astype(jnp.float32)).astype(jnp.bfloat16)


def dot3(a, b, dims):
    (ah, al), (bh, bl) = a, b
    one = functools.partial(
        lax.dot_general, dimension_numbers=(dims, ((), ())), preferred_element_type=jnp.float32
    )
    return one(ah, bh) + (one(ah, bl) + one(al, bh))


def dot_full(a, b, dims):
    return lax.dot_general(
        a, b, (dims, ((), ())), precision=lax.Precision.HIGHEST, preferred_element_type=jnp.float32
    )


def packed_blocks(m):
    return [
        (r, c)
        for r in range(0, m, PART)
        for c in range(0, r + PART, LANES)
    ]


def fibre_index():
    return lax.axis_index("fibre")


def place_rows(parts, high, low):
    rows = parts[0].shape[0]
    me = fibre_index()
    for k, part in enumerate(parts):
        at = pl.ds(pl.multiple_of((me ^ k) * rows, rows), rows)
        high[at, :], low[at, :] = split(part[...] if len(part.shape) == 2 else part[0])


def gram_kernel(scale, n, *refs):
    parts, (mine, theirs, high, low, packed) = refs[:n], refs[n:]
    m = high.shape[0]
    half = m // 2
    place_rows(parts, high, low)
    blocks = packed_blocks(m)
    for start in (0, half):
        rows, upto = slice(start, start + half), slice(0, start + half)
        g = dot3((high[rows, :], low[rows, :]), (high[upto, :], low[upto, :]), ((1,), (1,))) * scale
        for i, (r, c) in enumerate(blocks):
            if start <= r < start + half:
                packed[i * PART : (i + 1) * PART, :] = g[r - start : r - start + PART, c : c + LANES]
    me = fibre_index()
    piece = packed.shape[0] // n
    for k in range(0, n, 2):
        to = slice(k // 2 * piece, (k // 2 + 1) * piece)
        mine[to, :] = packed[pl.ds(pl.multiple_of(piece_of(me ^ k, n) * piece, SUB), piece), :]
        theirs[to, :] = packed[pl.ds(pl.multiple_of(piece_of(me ^ k ^ 1, n) * piece, SUB), piece), :]


def piece_of(device, n):
    return device


def gram_packed(parts, scale):
    rows, w = parts[0].shape
    n = len(parts)
    m = rows * n
    size = len(packed_blocks(m)) * PART
    half = jax.ShapeDtypeStruct((size // 2, LANES), jnp.float32)
    wide = jax.ShapeDtypeStruct((m, w), jnp.bfloat16)
    return pl.pallas_call(
        functools.partial(gram_kernel, scale, n),
        out_shape=[half, half, wide, wide],
        scratch_shapes=[pltpu.VMEM((size, LANES), jnp.float32)],
        compiler_params=pltpu.CompilerParams(vmem_limit_bytes=24 * MIB),
        cost_estimate=SHORT,
        name="gram",
    )(*parts)


def along_lanes(v, j):
    return jnp.broadcast_to(v[:, j : j + 1], (SUB, LANES))


def along_sublanes(v, s):
    return jnp.broadcast_to(v[s : s + 1, :], (SUB, LANES))


def factor_block(x, z):
    sub = lax.broadcasted_iota(jnp.int32, (SUB, LANES), 0)
    for g in range(len(x)):
        cols = [along_lanes(x[g], SUB * g + t) for t in range(SUB)]
        x_rows, z_rows, inverses, r = [], [], [], {}
        xg, zg = x[g], z[g]
        for t in range(SUB):
            inverse = lax.rsqrt(along_sublanes(cols[t], t))
            m = jnp.where(sub > t, cols[t] * inverse, 0.0)
            x_row, z_row = along_sublanes(xg, t) * inverse, along_sublanes(zg, t) * inverse
            xg = jnp.where(sub == t, x_row, xg - m * x_row)
            zg = jnp.where(sub == t, z_row, zg - m * z_row)
            for u in range(t + 1, SUB):
                r[t, u] = along_sublanes(cols[u], t) * inverse
                cols[u] = cols[u] - m * r[t, u]
            x_rows.append(x_row)
            z_rows.append(z_row)
            inverses.append(inverse)
        x[g], z[g] = xg, zg
        for h in range(g + 1, len(x)):
            cols = [along_lanes(x[h], SUB * g + t) for t in range(SUB)]
            for t in range(SUB):
                cols[t] = cols[t] * inverses[t]
                for u in range(t + 1, SUB):
                    cols[u] = cols[u] - cols[t] * r[t, u]
                x[h] = x[h] - cols[t] * x_rows[t]
                z[h] = z[h] - cols[t] * z_rows[t]
    return jnp.concatenate(x, 0), jnp.concatenate(z, 0)


def factor_kernel(m, n, *refs):
    pieces, (l_ref, w_ref, a_ref, packed) = refs[:n], refs[n:]
    piece = pieces[0].shape[0]
    me = fibre_index()
    for k, part in enumerate(pieces):
        packed[pl.ds(pl.multiple_of(piece_of(me ^ k, n) * piece, SUB), piece), :] = part[...]
    for i, (r, c) in enumerate(packed_blocks(m)):
        a_ref[r : r + PART, c : c + LANES] = packed[i * PART : (i + 1) * PART, :]
    l_ref[...] = jnp.zeros((m, m), jnp.float32)
    w_ref[...] = jnp.zeros((m, m), jnp.float32)
    row = lax.broadcasted_iota(jnp.int32, (LANES, LANES), 0)
    lane = lax.broadcasted_iota(jnp.int32, (LANES, LANES), 1)
    groups = range(0, LANES, SUB)
    for k in range(0, m, LANES):
        ks = slice(k, k + LANES)
        x = [a_ref[k + s : k + s + SUB, ks] for s in groups]
        z = [(lane[s : s + SUB] == row[s : s + SUB]).astype(jnp.float32) for s in groups]
        upper, inverse = factor_block(x, z)
        l_ref[ks, ks] = jnp.where(row >= lane, upper.T, 0.0)
        w_ref[ks, ks] = inverse
        if k + LANES < m:
            rest = slice(k + LANES, m)
            panel = dot_full(a_ref[rest, ks], inverse, ((1,), (1,)))
            l_ref[rest, ks] = panel
            a_ref[rest, rest] = a_ref[rest, rest] - dot_full(panel, panel, ((1,), (1,)))
    for i in range(LANES, m, LANES):
        rows = slice(i, i + LANES)
        acc = dot_full(l_ref[rows, 0:i], w_ref[0:i, 0:i], ((1,), (0,)))
        w_ref[rows, 0:i] = -dot_full(w_ref[rows, rows], acc, ((1,), (0,)))


def factor_and_inverse(pieces, m):
    n = len(pieces)
    return pl.pallas_call(
        functools.partial(factor_kernel, m, n),
        out_shape=[jax.ShapeDtypeStruct((m, m), jnp.float32)] * 2,
        scratch_shapes=[
            pltpu.VMEM((m, m), jnp.float32),
            pltpu.VMEM((n * pieces[0].shape[0], LANES), jnp.float32),
        ],
        compiler_params=pltpu.CompilerParams(vmem_limit_bytes=24 * MIB),
        cost_estimate=SHORT,
        name="factor",
    )(*pieces)


def rows_of(w_ref, wide, ks, rows):
    me = fibre_index()
    for i, k in enumerate(ks):
        piece = w_ref[pl.ds(pl.multiple_of((me ^ k) * rows, rows), rows), :]
        high, low = split(piece)
        for half, value in zip(wide, (high, low), strict=True):
            half[i * rows : (i + 1) * rows, :] = value


def send_kernel(ks, w_ref, high, low, *refs):
    outs, wide = refs[: len(ks)], refs[len(ks) :]
    rows, width = outs[0].shape
    rows_of(w_ref, wide, ks, rows)
    for start in range(0, width, width // 2):
        cols = slice(start, start + width // 2)
        solved = dot3((wide[0][...], wide[1][...]), (high[:, cols], low[:, cols]), ((1,), (0,)))
        for i, out in enumerate(outs):
            out[:, cols] = solved[i * rows : (i + 1) * rows]


def rows_to_send(w, high, low, ks, rows):
    m, width = high.shape
    return pl.pallas_call(
        functools.partial(send_kernel, ks),
        out_shape=[jax.ShapeDtypeStruct((rows, width), jnp.float32)] * len(ks),
        scratch_shapes=[pltpu.VMEM((len(ks) * rows, m), jnp.bfloat16)] * 2,
        compiler_params=pltpu.CompilerParams(vmem_limit_bytes=24 * MIB),
        cost_estimate=SHORT,
        name="send_rows",
    )(w, high, low)


def keep_kernel(n, w_ref, high, low, *refs):
    parts, outs, (twin_high, twin_low), wide = refs[:n], refs[n : n + 6], refs[n + 6 : n + 8], refs[n + 8 :]
    rows, width = outs[0].shape
    half = width // 2
    rows_of(w_ref, wide, (0, 1), rows)
    place_rows(parts, twin_high, twin_low)
    for (out, *near), h, l in ((outs[:3], high, low), (outs[3:], twin_high, twin_low)):
        for i in range(2):
            cols = slice(i * half, (i + 1) * half)
            solved = dot3((wide[0][...], wide[1][...]), (h[:, cols], l[:, cols]), ((1,), (0,)))
            out[:, cols] = solved[:rows]
            near[i][...] = solved[rows:]


def rows_to_keep(w, high, low, twin):
    m, width = high.shape
    n = len(twin)
    rows = m // n
    own = jax.ShapeDtypeStruct((rows, width), jnp.float32)
    near = jax.ShapeDtypeStruct((rows, width // 2), jnp.float32)
    return pl.pallas_call(
        functools.partial(keep_kernel, n),
        out_shape=[own, near, near, own, near, near],
        scratch_shapes=[pltpu.VMEM((m, width), jnp.bfloat16)] * 2 + [pltpu.VMEM((2 * rows, m), jnp.bfloat16)] * 2,
        compiler_params=pltpu.CompilerParams(vmem_limit_bytes=24 * MIB),
        cost_estimate=KEEP,
        name="keep_rows",
    )(w, high, low, *twin)


def permute(x, axis, bits):
    return lax.ppermute(x, axis, [(i, i ^ bits) for i in range(lax.axis_size(axis))])


def tree_sum(terms):
    while len(terms) > 1:
        terms = [a + b for a, b in zip(terms[::2], terms[1::2], strict=True)]
    return terms[0]


def after(x, *earlier):
    return lax.optimization_barrier((x, *earlier))[0]


def assemble_kernel(places, width, n_old, *refs):
    count = len(places)
    blocks, (out, sems) = refs[n_old : n_old + count], refs[n_old + count :]
    me = fibre_index()
    copies = []
    for i, ((k, start), block) in enumerate(zip(places, blocks, strict=True)):
        at = pl.multiple_of((me ^ k) * width, width) + start
        place = out.at[:, pl.ds(pl.multiple_of(at, LANES), block.shape[1])]
        copies.append(pltpu.make_async_copy(block, place, sems.at[i]))
    for copy in copies:
        copy.start()
    for copy in copies:
        copy.wait()


def assemble(blocks, rows, width, n, old=None):
    places = tuple(blocks)
    olds = () if old is None else (old,)
    return pl.pallas_call(
        functools.partial(assemble_kernel, places, width, len(olds)),
        out_shape=jax.ShapeDtypeStruct((rows, width * n), jnp.float32),
        in_specs=[pl.BlockSpec(memory_space=pl.ANY)] * (len(olds) + len(places)),
        out_specs=pl.BlockSpec(memory_space=pl.ANY),
        scratch_shapes=[pltpu.SemaphoreType.DMA((len(places),))],
        input_output_aliases={0: 0} if olds else {},
        compiler_params=pltpu.CompilerParams(vmem_limit_bytes=MIB),
        cost_estimate=SHORT,
        name="assemble",
    )(*olds, *blocks.values())


def local(tensor):
    n = lax.axis_size("fibre")
    groups = lax.axis_size("group")
    chips = n // 2
    me = lax.axis_index("fibre")
    rows, wide = tensor.shape
    m, width = rows * n, wide // n
    opposite = n - 2

    def block(x, j):
        return lax.dynamic_slice(x, (0, j * width), (rows, width))

    far = (opposite + 1, opposite)
    odd, even = list(range(3, n - 2, 2)), list(range(2, n - 2, 2))
    blocks = {k: block(tensor, me ^ k) for k in far}
    rest = after(tensor, *blocks.values())
    blocks |= {k: block(rest, me ^ k) for k in range(n - 2)}
    parts = [permute(blocks[k], "fibre", k) if k else blocks[0] for k in range(n)]
    twin = [block(rest, me ^ k ^ opposite) for k in range(opposite)] + [None, None]
    mine, theirs, high, low = gram_packed(parts, 1.0 / (width * n * groups))
    mine = (mine + permute(theirs, "fibre", 1)).reshape(chips, -1, LANES)
    piece = tree_sum([mine[k] if k == 0 else permute(mine[k], "fibre", 2 * k) for k in range(chips)])
    for k in even:
        twin[k] = permute(after(twin[k], piece), "fibre", k)
    piece = tree_sum([piece if k == 0 else permute(piece, "group", k) for k in range(groups)])
    piece, *arrived = lax.optimization_barrier((piece, *[twin[k] for k in even]))
    for k, x in zip(even, arrived, strict=True):
        twin[k] = x
    pieces = [None] * n
    for k in range(chips):
        pieces[2 * k] = piece if k == 0 else permute(piece, "fibre", 2 * k)
        pieces[2 * k + 1] = permute(pieces[2 * k], "fibre", 1)
    own = after(jnp.stack([blocks[0], blocks[1]]), *pieces[2::2])
    twin[opposite] = permute(own, "fibre", opposite)
    for k in (*odd, 1):
        twin[k] = permute(after(twin[k], *pieces[3::2]), "fibre", k)
    factor, inverse = factor_and_inverse(pieces, m)
    ks = tuple(range(2, n - 2))
    solved = rows_to_send(inverse, high, low, ks, rows)
    sent = {k: permute(x, "fibre", k) for k, x in zip(ks, solved, strict=True)}
    twin[opposite] = after(twin[opposite], solved[0])
    twin[opposite + 1] = permute(twin[opposite][1], "fibre", 1)
    kept = rows_to_keep(inverse, high, low, twin)
    here = {(0, 0): kept[0], (opposite, 0): kept[3]}
    for k, near in ((1, kept[1:3]), (opposite + 1, kept[4:])):
        for i, x in enumerate(near):
            here[k, i * width // 2] = permute(x, "fibre", 1)
    basis = assemble(here | {(k, 0): sent[k] for k in even}, rows, width, n)
    if odd:
        basis = assemble({(k, 0): sent[k] for k in odd}, rows, width, n, basis)
    return (basis, factor)


def solution(mesh):
    return jax.shard_map(
        local,
        mesh=mesh,
        in_specs=(P("fibre", "group"),),
        out_specs=(P("fibre", "group"), P()),
        check_vma=False,
    )
```

```python
import functools

import jax
import jax.numpy as jnp
from jax import lax
from jax.experimental import pallas as pl
from jax.experimental.pallas import tpu as pltpu
from jax.sharding import PartitionSpec as P

LANES = 128
SUB = 8
PART = 32
MIB = 1024 * 1024
SHORT = pl.CostEstimate(flops=1024, bytes_accessed=1024, transcendentals=0)
KEEP = SHORT


def split(x):
    high = x.astype(jnp.bfloat16)
    return high, (x - high.astype(jnp.float32)).astype(jnp.bfloat16)


def dot3(a, b, dims):
    (ah, al), (bh, bl) = a, b
    one = functools.partial(
        lax.dot_general, dimension_numbers=(dims, ((), ())), preferred_element_type=jnp.float32
    )
    return one(ah, bh) + (one(ah, bl) + one(al, bh))


def dot_full(a, b, dims):
    return lax.dot_general(
        a, b, (dims, ((), ())), precision=lax.Precision.HIGHEST, preferred_element_type=jnp.float32
    )


def packed_blocks(m):
    return [
        (r, c)
        for r in range(0, m, PART)
        for c in range(0, r + PART, LANES)
    ]


def fibre_index():
    return lax.axis_index("fibre")


def place_rows(parts, high, low):
    rows = parts[0].shape[0]
    me = fibre_index()
    for k, part in enumerate(parts):
        at = pl.ds(pl.multiple_of((me ^ k) * rows, rows), rows)
        high[at, :], low[at, :] = split(part[...] if len(part.shape) == 2 else part[0])


def gram_kernel(scale, n, *refs):
    parts, (mine, theirs, high, low, packed) = refs[:n], refs[n:]
    m = high.shape[0]
    half = m // 2
    place_rows(parts, high, low)
    blocks = packed_blocks(m)
    for start in (0, half):
        rows, upto = slice(start, start + half), slice(0, start + half)
        g = dot3((high[rows, :], low[rows, :]), (high[upto, :], low[upto, :]), ((1,), (1,))) * scale
        for i, (r, c) in enumerate(blocks):
            if start <= r < start + half:
                packed[i * PART : (i + 1) * PART, :] = g[r - start : r - start + PART, c : c + LANES]
    me = fibre_index()
    piece = packed.shape[0] // n
    for k in range(0, n, 2):
        to = slice(k // 2 * piece, (k // 2 + 1) * piece)
        mine[to, :] = packed[pl.ds(pl.multiple_of(piece_of(me ^ k, n) * piece, SUB), piece), :]
        theirs[to, :] = packed[pl.ds(pl.multiple_of(piece_of(me ^ k ^ 1, n) * piece, SUB), piece), :]


def piece_of(device, n):
    return device


def gram_packed(parts, scale):
    rows, w = parts[0].shape
    n = len(parts)
    m = rows * n
    size = len(packed_blocks(m)) * PART
    half = jax.ShapeDtypeStruct((size // 2, LANES), jnp.float32)
    wide = jax.ShapeDtypeStruct((m, w), jnp.bfloat16)
    return pl.pallas_call(
        functools.partial(gram_kernel, scale, n),
        out_shape=[half, half, wide, wide],
        scratch_shapes=[pltpu.VMEM((size, LANES), jnp.float32)],
        compiler_params=pltpu.CompilerParams(vmem_limit_bytes=24 * MIB),
        cost_estimate=SHORT,
        name="gram",
    )(*parts)


def along_lanes(v, j):
    return jnp.broadcast_to(v[:, j : j + 1], (SUB, LANES))


def along_sublanes(v, s):
    return jnp.broadcast_to(v[s : s + 1, :], (SUB, LANES))


def factor_block(x, z):
    sub = lax.broadcasted_iota(jnp.int32, (SUB, LANES), 0)
    for g in range(len(x)):
        cols = [along_lanes(x[g], SUB * g + t) for t in range(SUB)]
        x_rows, z_rows, inverses, r = [], [], [], {}
        xg, zg = x[g], z[g]
        for t in range(SUB):
            inverse = lax.rsqrt(along_sublanes(cols[t], t))
            m = jnp.where(sub > t, cols[t] * inverse, 0.0)
            x_row, z_row = along_sublanes(xg, t) * inverse, along_sublanes(zg, t) * inverse
            xg = jnp.where(sub == t, x_row, xg - m * x_row)
            zg = jnp.where(sub == t, z_row, zg - m * z_row)
            for u in range(t + 1, SUB):
                r[t, u] = along_sublanes(cols[u], t) * inverse
                cols[u] = cols[u] - m * r[t, u]
            x_rows.append(x_row)
            z_rows.append(z_row)
            inverses.append(inverse)
        x[g], z[g] = xg, zg
        for h in range(g + 1, len(x)):
            cols = [along_lanes(x[h], SUB * g + t) for t in range(SUB)]
            for t in range(SUB):
                cols[t] = cols[t] * inverses[t]
                for u in range(t + 1, SUB):
                    cols[u] = cols[u] - cols[t] * r[t, u]
                x[h] = x[h] - cols[t] * x_rows[t]
                z[h] = z[h] - cols[t] * z_rows[t]
    return jnp.concatenate(x, 0), jnp.concatenate(z, 0)


def factor_kernel(m, n, *refs):
    pieces, (l_ref, w_ref, a_ref, packed) = refs[:n], refs[n:]
    piece = pieces[0].shape[0]
    me = fibre_index()
    for k, part in enumerate(pieces):
        packed[pl.ds(pl.multiple_of(piece_of(me ^ k, n) * piece, SUB), piece), :] = part[...]
    for i, (r, c) in enumerate(packed_blocks(m)):
        a_ref[r : r + PART, c : c + LANES] = packed[i * PART : (i + 1) * PART, :]
    l_ref[...] = jnp.zeros((m, m), jnp.float32)
    w_ref[...] = jnp.zeros((m, m), jnp.float32)
    row = lax.broadcasted_iota(jnp.int32, (LANES, LANES), 0)
    lane = lax.broadcasted_iota(jnp.int32, (LANES, LANES), 1)
    groups = range(0, LANES, SUB)
    for k in range(0, m, LANES):
        ks = slice(k, k + LANES)
        x = [a_ref[k + s : k + s + SUB, ks] for s in groups]
        z = [(lane[s : s + SUB] == row[s : s + SUB]).astype(jnp.float32) for s in groups]
        upper, inverse = factor_block(x, z)
        l_ref[ks, ks] = jnp.where(row >= lane, upper.T, 0.0)
        w_ref[ks, ks] = inverse
        if k + LANES < m:
            rest = slice(k + LANES, m)
            panel = dot_full(a_ref[rest, ks], inverse, ((1,), (1,)))
            l_ref[rest, ks] = panel
            a_ref[rest, rest] = a_ref[rest, rest] - dot_full(panel, panel, ((1,), (1,)))
    for i in range(LANES, m, LANES):
        rows = slice(i, i + LANES)
        acc = dot_full(l_ref[rows, 0:i], w_ref[0:i, 0:i], ((1,), (0,)))
        w_ref[rows, 0:i] = -dot_full(w_ref[rows, rows], acc, ((1,), (0,)))


def factor_and_inverse(pieces, m):
    n = len(pieces)
    return pl.pallas_call(
        functools.partial(factor_kernel, m, n),
        out_shape=[jax.ShapeDtypeStruct((m, m), jnp.float32)] * 2,
        scratch_shapes=[
            pltpu.VMEM((m, m), jnp.float32),
            pltpu.VMEM((n * pieces[0].shape[0], LANES), jnp.float32),
        ],
        compiler_params=pltpu.CompilerParams(vmem_limit_bytes=24 * MIB),
        cost_estimate=SHORT,
        name="factor",
    )(*pieces)


def rows_of(w_ref, wide, ks, rows):
    me = fibre_index()
    for i, k in enumerate(ks):
        piece = w_ref[pl.ds(pl.multiple_of((me ^ k) * rows, rows), rows), :]
        high, low = split(piece)
        for half, value in zip(wide, (high, low), strict=True):
            half[i * rows : (i + 1) * rows, :] = value


def send_kernel(ks, w_ref, high, low, *refs):
    outs, wide = refs[: len(ks)], refs[len(ks) :]
    rows, width = outs[0].shape
    rows_of(w_ref, wide, ks, rows)
    for start in range(0, width, width // 2):
        cols = slice(start, start + width // 2)
        solved = dot3((wide[0][...], wide[1][...]), (high[:, cols], low[:, cols]), ((1,), (0,)))
        for i, out in enumerate(outs):
            out[:, cols] = solved[i * rows : (i + 1) * rows]


def rows_to_send(w, high, low, ks, rows):
    m, width = high.shape
    return pl.pallas_call(
        functools.partial(send_kernel, ks),
        out_shape=[jax.ShapeDtypeStruct((rows, width), jnp.float32)] * len(ks),
        scratch_shapes=[pltpu.VMEM((len(ks) * rows, m), jnp.bfloat16)] * 2,
        compiler_params=pltpu.CompilerParams(vmem_limit_bytes=24 * MIB),
        cost_estimate=SHORT,
        name="send_rows",
    )(w, high, low)


def keep_kernel(n, w_ref, high, low, *refs):
    parts, outs, (twin_high, twin_low), wide = refs[:n], refs[n : n + 6], refs[n + 6 : n + 8], refs[n + 8 :]
    rows, width = outs[0].shape
    half = width // 2
    rows_of(w_ref, wide, (0, 1), rows)
    place_rows(parts, twin_high, twin_low)
    for (out, *near), h, l in ((outs[:3], high, low), (outs[3:], twin_high, twin_low)):
        for i in range(2):
            cols = slice(i * half, (i + 1) * half)
            solved = dot3((wide[0][...], wide[1][...]), (h[:, cols], l[:, cols]), ((1,), (0,)))
            out[:, cols] = solved[:rows]
            near[i][...] = solved[rows:]


def rows_to_keep(w, high, low, twin):
    m, width = high.shape
    n = len(twin)
    rows = m // n
    own = jax.ShapeDtypeStruct((rows, width), jnp.float32)
    near = jax.ShapeDtypeStruct((rows, width // 2), jnp.float32)
    return pl.pallas_call(
        functools.partial(keep_kernel, n),
        out_shape=[own, near, near, own, near, near],
        scratch_shapes=[pltpu.VMEM((m, width), jnp.bfloat16)] * 2 + [pltpu.VMEM((2 * rows, m), jnp.bfloat16)] * 2,
        compiler_params=pltpu.CompilerParams(vmem_limit_bytes=24 * MIB),
        cost_estimate=KEEP,
        name="keep_rows",
    )(w, high, low, *twin)


def permute(x, axis, bits):
    return lax.ppermute(x, axis, [(i, i ^ bits) for i in range(lax.axis_size(axis))])


def tree_sum(terms):
    while len(terms) > 1:
        terms = [a + b for a, b in zip(terms[::2], terms[1::2], strict=True)]
    return terms[0]


def after(x, *earlier):
    return lax.optimization_barrier((x, *earlier))[0]


def assemble_kernel(places, width, n_old, *refs):
    count = len(places)
    blocks, (out, sems) = refs[n_old : n_old + count], refs[n_old + count :]
    me = fibre_index()
    copies = []
    for i, ((k, start), block) in enumerate(zip(places, blocks, strict=True)):
        at = pl.multiple_of((me ^ k) * width, width) + start
        place = out.at[:, pl.ds(pl.multiple_of(at, LANES), block.shape[1])]
        copies.append(pltpu.make_async_copy(block, place, sems.at[i]))
    for copy in copies:
        copy.start()
    for copy in copies:
        copy.wait()


def assemble(blocks, rows, width, n, old=None):
    places = tuple(blocks)
    olds = () if old is None else (old,)
    return pl.pallas_call(
        functools.partial(assemble_kernel, places, width, len(olds)),
        out_shape=jax.ShapeDtypeStruct((rows, width * n), jnp.float32),
        in_specs=[pl.BlockSpec(memory_space=pl.ANY)] * (len(olds) + len(places)),
        out_specs=pl.BlockSpec(memory_space=pl.ANY),
        scratch_shapes=[pltpu.SemaphoreType.DMA((len(places),))],
        input_output_aliases={0: 0} if olds else {},
        compiler_params=pltpu.CompilerParams(vmem_limit_bytes=MIB),
        cost_estimate=SHORT,
        name="assemble",
    )(*olds, *blocks.values())


def local(tensor):
    n = lax.axis_size("fibre")
    groups = lax.axis_size("group")
    chips = n // 2
    me = lax.axis_index("fibre")
    rows, wide = tensor.shape
    m, width = rows * n, wide // n
    opposite = n - 2

    def block(x, j):
        return lax.dynamic_slice(x, (0, j * width), (rows, width))

    far = opposite + 1
    odd, even = list(range(3, n - 2, 2)), list(range(2, n - 2, 2))
    blocks = {far: block(tensor, me ^ far)}
    rest = after(tensor, blocks[far])
    blocks |= {k: block(rest, me ^ k) for k in range(far)}
    parts = [permute(blocks[k], "fibre", k) if k else blocks[0] for k in range(n)]
    twin = [block(rest, me ^ k ^ opposite) for k in range(opposite)] + [None, None]
    mine, theirs, high, low = gram_packed(parts, 1.0 / (width * n * groups))
    mine = (mine + permute(theirs, "fibre", 1)).reshape(chips, -1, LANES)
    terms = [mine[k] if k == 0 else permute(mine[k], "fibre", 2 * k) for k in range(chips)]
    for k in even:
        twin[k] = permute(after(twin[k], terms[-1]), "fibre", k)
    piece = tree_sum(terms)
    piece = tree_sum([piece if k == 0 else permute(piece, "group", k) for k in range(groups)])
    piece, *arrived = lax.optimization_barrier((piece, *[twin[k] for k in even]))
    for k, x in zip(even, arrived, strict=True):
        twin[k] = x
    pieces = [None] * n
    for k in range(chips):
        pieces[2 * k] = piece if k == 0 else permute(piece, "fibre", 2 * k)
        pieces[2 * k + 1] = permute(pieces[2 * k], "fibre", 1)
    own = after(jnp.stack([blocks[0], blocks[1]]), *pieces[2::2])
    twin[opposite] = permute(own, "fibre", opposite)
    for k in (*odd, 1):
        twin[k] = permute(after(twin[k], *pieces[3::2]), "fibre", k)
    factor, inverse = factor_and_inverse(pieces, m)
    ks = tuple(range(2, n - 2))
    solved = rows_to_send(inverse, high, low, ks, rows)
    sent = {k: permute(x, "fibre", k) for k, x in zip(ks, solved, strict=True)}
    twin[opposite] = after(twin[opposite], solved[0])
    twin[opposite + 1] = permute(twin[opposite][1], "fibre", 1)
    kept = rows_to_keep(inverse, high, low, twin)
    here = {(0, 0): kept[0], (opposite, 0): kept[3]}
    for k, near in ((1, kept[1:3]), (opposite + 1, kept[4:])):
        for i, x in enumerate(near):
            here[k, i * width // 2] = permute(x, "fibre", 1)
    basis = assemble(here | {(k, 0): sent[k] for k in even}, rows, width, n)
    if odd:
        basis = assemble({(k, 0): sent[k] for k in odd}, rows, width, n, basis)
    return (basis, factor)


def solution(mesh):
    return jax.shard_map(
        local,
        mesh=mesh,
        in_specs=(P("fibre", "group"),),
        out_specs=(P("fibre", "group"), P()),
        check_vma=False,
    )
```

```python
import functools

import jax
import jax.numpy as jnp
from jax import lax
from jax.experimental import pallas as pl
from jax.experimental.pallas import tpu as pltpu
from jax.sharding import PartitionSpec as P

LANES = 128
SUB = 8
PART = 32
MIB = 1024 * 1024
SHORT = pl.CostEstimate(flops=1024, bytes_accessed=1024, transcendentals=0)
KEEP = SHORT


def split(x):
    high = x.astype(jnp.bfloat16)
    return high, (x - high.astype(jnp.float32)).astype(jnp.bfloat16)


def dot3(a, b, dims):
    (ah, al), (bh, bl) = a, b
    one = functools.partial(
        lax.dot_general, dimension_numbers=(dims, ((), ())), preferred_element_type=jnp.float32
    )
    return one(ah, bh) + (one(ah, bl) + one(al, bh))


def dot_full(a, b, dims):
    return lax.dot_general(
        a, b, (dims, ((), ())), precision=lax.Precision.HIGHEST, preferred_element_type=jnp.float32
    )


def packed_blocks(m):
    return [
        (r, c)
        for r in range(0, m, PART)
        for c in range(0, r + PART, LANES)
    ]


def fibre_index():
    return lax.axis_index("fibre")


def place_rows(parts, high, low):
    rows = parts[0].shape[0]
    me = fibre_index()
    for k, part in enumerate(parts):
        at = pl.ds(pl.multiple_of((me ^ k) * rows, rows), rows)
        high[at, :], low[at, :] = split(part[...] if len(part.shape) == 2 else part[0])


def gram_kernel(scale, n, *refs):
    parts, (mine, theirs, high, low, packed) = refs[:n], refs[n:]
    m = high.shape[0]
    half = m // 2
    place_rows(parts, high, low)
    blocks = packed_blocks(m)
    for start in (0, half):
        rows, upto = slice(start, start + half), slice(0, start + half)
        g = dot3((high[rows, :], low[rows, :]), (high[upto, :], low[upto, :]), ((1,), (1,))) * scale
        for i, (r, c) in enumerate(blocks):
            if start <= r < start + half:
                packed[i * PART : (i + 1) * PART, :] = g[r - start : r - start + PART, c : c + LANES]
    me = fibre_index()
    piece = packed.shape[0] // n
    for k in range(0, n, 2):
        to = slice(k // 2 * piece, (k // 2 + 1) * piece)
        mine[to, :] = packed[pl.ds(pl.multiple_of(piece_of(me ^ k, n) * piece, SUB), piece), :]
        theirs[to, :] = packed[pl.ds(pl.multiple_of(piece_of(me ^ k ^ 1, n) * piece, SUB), piece), :]


def piece_of(device, n):
    return device


def gram_packed(parts, scale):
    rows, w = parts[0].shape
    n = len(parts)
    m = rows * n
    size = len(packed_blocks(m)) * PART
    half = jax.ShapeDtypeStruct((size // 2, LANES), jnp.float32)
    wide = jax.ShapeDtypeStruct((m, w), jnp.bfloat16)
    return pl.pallas_call(
        functools.partial(gram_kernel, scale, n),
        out_shape=[half, half, wide, wide],
        scratch_shapes=[pltpu.VMEM((size, LANES), jnp.float32)],
        compiler_params=pltpu.CompilerParams(vmem_limit_bytes=24 * MIB),
        cost_estimate=SHORT,
        name="gram",
    )(*parts)


def along_lanes(v, j):
    return jnp.broadcast_to(v[:, j : j + 1], (SUB, LANES))


def along_sublanes(ref, s):
    return jnp.broadcast_to(ref[s : s + 1, :], (SUB, LANES))


def factor_block(x, z, x_ref, z_ref, c_ref):
    sub = lax.broadcasted_iota(jnp.int32, (SUB, LANES), 0)
    eight = range(SUB)
    for g in range(len(x)):
        at = SUB * g
        x_ref[at : at + SUB, :], z_ref[at : at + SUB, :] = x[g], z[g]
        for t in eight:
            c_ref[SUB * (at + t) : SUB * (at + t + 1), :] = along_lanes(x[g], at + t)
        d = {(t, u): along_sublanes(c_ref, SUB * (at + u) + t) for u in eight for t in range(u + 1)}
        x_rows = [along_sublanes(x_ref, at + t) for t in eight]
        z_rows = [along_sublanes(z_ref, at + t) for t in eight]
        scale, r = [], {}
        for t in eight:
            scale.append(lax.rsqrt(d[t, t]))
            inverse = scale[t] * scale[t]
            x_rows[t], z_rows[t] = x_rows[t] * scale[t], z_rows[t] * scale[t]
            for u in range(t + 1, SUB):
                for v in range(t + 1, u + 1):
                    d[v, u] = d[v, u] - (d[t, v] * d[t, u]) * inverse
                r[t, u] = d[t, u] * scale[t]
                x_rows[u] = x_rows[u] - r[t, u] * x_rows[t]
                z_rows[u] = z_rows[u] - r[t, u] * z_rows[t]
        x[g], z[g] = x_rows[0], z_rows[0]
        for t in range(1, SUB):
            x[g], z[g] = jnp.where(sub == t, x_rows[t], x[g]), jnp.where(sub == t, z_rows[t], z[g])
        if g + 1 < len(x):
            cols = [along_lanes(x[g + 1], at + t) for t in eight]
            for t in eight:
                cols[t] = cols[t] * scale[t]
                for u in range(t + 1, SUB):
                    cols[u] = cols[u] - cols[t] * r[t, u]
                x[g + 1] = x[g + 1] - cols[t] * x_rows[t]
                z[g + 1] = z[g + 1] - cols[t] * z_rows[t]
        for t in reversed(eight):
            for u in range(t + 1, SUB):
                x_rows[t] = x_rows[t] - r[t, u] * x_rows[u]
                z_rows[t] = z_rows[t] - r[t, u] * z_rows[u]
            x_rows[t], z_rows[t] = x_rows[t] * scale[t], z_rows[t] * scale[t]
        for h in range(g + 2, len(x)):
            for t in eight:
                col = along_lanes(x[h], at + t)
                if t == 0:
                    x_sum, z_sum = col * x_rows[t], col * z_rows[t]
                else:
                    x_sum, z_sum = x_sum + col * x_rows[t], z_sum + col * z_rows[t]
            x[h], z[h] = x[h] - x_sum, z[h] - z_sum
    return jnp.concatenate(x, 0), jnp.concatenate(z, 0)


def factor_kernel(m, n, *refs):
    pieces, (l_ref, w_ref, a_ref, packed, *spare) = refs[:n], refs[n:]
    piece = pieces[0].shape[0]
    me = fibre_index()
    for k, part in enumerate(pieces):
        packed[pl.ds(pl.multiple_of(piece_of(me ^ k, n) * piece, SUB), piece), :] = part[...]
    for i, (r, c) in enumerate(packed_blocks(m)):
        a_ref[r : r + PART, c : c + LANES] = packed[i * PART : (i + 1) * PART, :]
    l_ref[...] = jnp.zeros((m, m), jnp.float32)
    w_ref[...] = jnp.zeros((m, m), jnp.float32)
    row = lax.broadcasted_iota(jnp.int32, (LANES, LANES), 0)
    lane = lax.broadcasted_iota(jnp.int32, (LANES, LANES), 1)
    groups = range(0, LANES, SUB)
    for k in range(0, m, LANES):
        ks = slice(k, k + LANES)
        x = [a_ref[k + s : k + s + SUB, ks] for s in groups]
        z = [(lane[s : s + SUB] == row[s : s + SUB]).astype(jnp.float32) for s in groups]
        upper, inverse = factor_block(x, z, *spare)
        l_ref[ks, ks] = jnp.where(row >= lane, upper.T, 0.0)
        w_ref[ks, ks] = inverse
        if k + LANES < m:
            rest = slice(k + LANES, m)
            panel = dot_full(a_ref[rest, ks], inverse, ((1,), (1,)))
            l_ref[rest, ks] = panel
            a_ref[rest, rest] = a_ref[rest, rest] - dot_full(panel, panel, ((1,), (1,)))
    for i in range(LANES, m, LANES):
        rows = slice(i, i + LANES)
        acc = dot_full(l_ref[rows, 0:i], w_ref[0:i, 0:i], ((1,), (0,)))
        w_ref[rows, 0:i] = -dot_full(w_ref[rows, rows], acc, ((1,), (0,)))


def factor_and_inverse(pieces, m):
    n = len(pieces)
    return pl.pallas_call(
        functools.partial(factor_kernel, m, n),
        out_shape=[jax.ShapeDtypeStruct((m, m), jnp.float32)] * 2,
        scratch_shapes=[
            pltpu.VMEM((m, m), jnp.float32),
            pltpu.VMEM((n * pieces[0].shape[0], LANES), jnp.float32),
            pltpu.VMEM((LANES, LANES), jnp.float32),
            pltpu.VMEM((LANES, LANES), jnp.float32),
            pltpu.VMEM((LANES * SUB, LANES), jnp.float32),
        ],
        compiler_params=pltpu.CompilerParams(vmem_limit_bytes=24 * MIB),
        cost_estimate=SHORT,
        name="factor",
    )(*pieces)


def rows_of(w_ref, wide, ks, rows):
    me = fibre_index()
    for i, k in enumerate(ks):
        piece = w_ref[pl.ds(pl.multiple_of((me ^ k) * rows, rows), rows), :]
        high, low = split(piece)
        for half, value in zip(wide, (high, low), strict=True):
            half[i * rows : (i + 1) * rows, :] = value


def send_kernel(ks, w_ref, high, low, *refs):
    outs, wide = refs[: len(ks)], refs[len(ks) :]
    rows, width = outs[0].shape
    rows_of(w_ref, wide, ks, rows)
    for start in range(0, width, width // 2):
        cols = slice(start, start + width // 2)
        solved = dot3((wide[0][...], wide[1][...]), (high[:, cols], low[:, cols]), ((1,), (0,)))
        for i, out in enumerate(outs):
            out[:, cols] = solved[i * rows : (i + 1) * rows]


def rows_to_send(w, high, low, ks, rows):
    m, width = high.shape
    return pl.pallas_call(
        functools.partial(send_kernel, ks),
        out_shape=[jax.ShapeDtypeStruct((rows, width), jnp.float32)] * len(ks),
        scratch_shapes=[pltpu.VMEM((len(ks) * rows, m), jnp.bfloat16)] * 2,
        compiler_params=pltpu.CompilerParams(vmem_limit_bytes=24 * MIB),
        cost_estimate=SHORT,
        name="send_rows",
    )(w, high, low)


def keep_kernel(n, w_ref, high, low, *refs):
    parts, outs, (twin_high, twin_low), wide = refs[:n], refs[n : n + 6], refs[n + 6 : n + 8], refs[n + 8 :]
    rows, width = outs[0].shape
    half = width // 2
    rows_of(w_ref, wide, (0, 1), rows)
    place_rows(parts, twin_high, twin_low)
    for (out, *near), h, l in ((outs[:3], high, low), (outs[3:], twin_high, twin_low)):
        for i in range(2):
            cols = slice(i * half, (i + 1) * half)
            solved = dot3((wide[0][...], wide[1][...]), (h[:, cols], l[:, cols]), ((1,), (0,)))
            out[:, cols] = solved[:rows]
            near[i][...] = solved[rows:]


def rows_to_keep(w, high, low, twin):
    m, width = high.shape
    n = len(twin)
    rows = m // n
    own = jax.ShapeDtypeStruct((rows, width), jnp.float32)
    near = jax.ShapeDtypeStruct((rows, width // 2), jnp.float32)
    return pl.pallas_call(
        functools.partial(keep_kernel, n),
        out_shape=[own, near, near, own, near, near],
        scratch_shapes=[pltpu.VMEM((m, width), jnp.bfloat16)] * 2 + [pltpu.VMEM((2 * rows, m), jnp.bfloat16)] * 2,
        compiler_params=pltpu.CompilerParams(vmem_limit_bytes=24 * MIB),
        cost_estimate=KEEP,
        name="keep_rows",
    )(w, high, low, *twin)


def permute(x, axis, bits):
    return lax.ppermute(x, axis, [(i, i ^ bits) for i in range(lax.axis_size(axis))])


def tree_sum(terms):
    while len(terms) > 1:
        terms = [a + b for a, b in zip(terms[::2], terms[1::2], strict=True)]
    return terms[0]


def after(x, *earlier):
    return lax.optimization_barrier((x, *earlier))[0]


def assemble_kernel(places, width, n_old, *refs):
    count = len(places)
    blocks, (out, sems) = refs[n_old : n_old + count], refs[n_old + count :]
    me = fibre_index()
    copies = []
    for i, ((k, start), block) in enumerate(zip(places, blocks, strict=True)):
        at = pl.multiple_of((me ^ k) * width, width) + start
        place = out.at[:, pl.ds(pl.multiple_of(at, LANES), block.shape[1])]
        copies.append(pltpu.make_async_copy(block, place, sems.at[i]))
    for copy in copies:
        copy.start()
    for copy in copies:
        copy.wait()


def assemble(blocks, rows, width, n, old=None):
    places = tuple(blocks)
    olds = () if old is None else (old,)
    return pl.pallas_call(
        functools.partial(assemble_kernel, places, width, len(olds)),
        out_shape=jax.ShapeDtypeStruct((rows, width * n), jnp.float32),
        in_specs=[pl.BlockSpec(memory_space=pl.ANY)] * (len(olds) + len(places)),
        out_specs=pl.BlockSpec(memory_space=pl.ANY),
        scratch_shapes=[pltpu.SemaphoreType.DMA((len(places),))],
        input_output_aliases={0: 0} if olds else {},
        compiler_params=pltpu.CompilerParams(vmem_limit_bytes=MIB),
        cost_estimate=SHORT,
        name="assemble",
    )(*olds, *blocks.values())


def local(tensor):
    n = lax.axis_size("fibre")
    groups = lax.axis_size("group")
    chips = n // 2
    me = lax.axis_index("fibre")
    rows, wide = tensor.shape
    m, width = rows * n, wide // n
    opposite = n - 2

    def block(x, j):
        return lax.dynamic_slice(x, (0, j * width), (rows, width))

    far = opposite + 1
    odd, even = list(range(3, n - 2, 2)), list(range(2, n - 2, 2))
    blocks = {far: block(tensor, me ^ far)}
    rest = after(tensor, blocks[far])
    blocks |= {k: block(rest, me ^ k) for k in range(far)}
    parts = [permute(blocks[k], "fibre", k) if k else blocks[0] for k in range(n)]
    twin = [block(rest, me ^ k ^ opposite) for k in range(opposite)] + [None, None]
    mine, theirs, high, low = gram_packed(parts, 1.0 / (width * n * groups))
    mine = (mine + permute(theirs, "fibre", 1)).reshape(chips, -1, LANES)
    terms = [mine[k] if k == 0 else permute(mine[k], "fibre", 2 * k) for k in range(chips)]
    for k in even:
        twin[k] = permute(after(twin[k], terms[-1]), "fibre", k)
    piece = tree_sum(terms)
    piece = tree_sum([piece if k == 0 else permute(piece, "group", k) for k in range(groups)])
    piece, *arrived = lax.optimization_barrier((piece, *[twin[k] for k in even]))
    for k, x in zip(even, arrived, strict=True):
        twin[k] = x
    pieces = [None] * n
    for k in range(chips):
        pieces[2 * k] = piece if k == 0 else permute(piece, "fibre", 2 * k)
        pieces[2 * k + 1] = permute(pieces[2 * k], "fibre", 1)
    own = after(jnp.stack([blocks[0], blocks[1]]), *pieces[2::2])
    twin[opposite] = permute(own, "fibre", opposite)
    for k in (*odd, 1):
        twin[k] = permute(after(twin[k], *pieces[3::2]), "fibre", k)
    factor, inverse = factor_and_inverse(pieces, m)
    ks = tuple(range(2, n - 2))
    solved = rows_to_send(inverse, high, low, ks, rows)
    sent = {k: permute(x, "fibre", k) for k, x in zip(ks, solved, strict=True)}
    twin[opposite] = after(twin[opposite], solved[0])
    twin[opposite + 1] = permute(twin[opposite][1], "fibre", 1)
    kept = rows_to_keep(inverse, high, low, twin)
    here = {(0, 0): kept[0], (opposite, 0): kept[3]}
    for k, near in ((1, kept[1:3]), (opposite + 1, kept[4:])):
        for i, x in enumerate(near):
            here[k, i * width // 2] = permute(x, "fibre", 1)
    basis = assemble(here | {(k, 0): sent[k] for k in even}, rows, width, n)
    if odd:
        basis = assemble({(k, 0): sent[k] for k in odd}, rows, width, n, basis)
    return (basis, factor)


def solution(mesh):
    return jax.shard_map(
        local,
        mesh=mesh,
        in_specs=(P("fibre", "group"),),
        out_specs=(P("fibre", "group"), P()),
        check_vma=False,
    )
```

```python
import functools

import jax
import jax.numpy as jnp
from jax import lax
from jax.experimental import pallas as pl
from jax.experimental.pallas import tpu as pltpu
from jax.sharding import PartitionSpec as P

LANES = 128
SUB = 8
PART = 32
MIB = 1024 * 1024
SHORT = pl.CostEstimate(flops=1024, bytes_accessed=1024, transcendentals=0)
KEEP = SHORT


def split(x):
    high = x.astype(jnp.bfloat16)
    return high, (x - high.astype(jnp.float32)).astype(jnp.bfloat16)


def dot3(a, b, dims):
    (ah, al), (bh, bl) = a, b
    one = functools.partial(
        lax.dot_general, dimension_numbers=(dims, ((), ())), preferred_element_type=jnp.float32
    )
    return one(ah, bh) + (one(ah, bl) + one(al, bh))


def dot_full(a, b, dims):
    return lax.dot_general(
        a, b, (dims, ((), ())), precision=lax.Precision.HIGHEST, preferred_element_type=jnp.float32
    )


def packed_blocks(m):
    return [
        (r, c)
        for r in range(0, m, PART)
        for c in range(0, r + PART, LANES)
    ]


def fibre_index():
    return lax.axis_index("fibre")


def place_rows(parts, high, low):
    rows = parts[0].shape[0]
    me = fibre_index()
    for k, part in enumerate(parts):
        at = pl.ds(pl.multiple_of((me ^ k) * rows, rows), rows)
        high[at, :], low[at, :] = split(part[...] if len(part.shape) == 2 else part[0])


def split_kernel(*refs):
    parts, (high, low) = refs[:-2], refs[-2:]
    rows = parts[0].shape[0]
    for i, part in enumerate(parts):
        at = slice(i * rows, (i + 1) * rows)
        high[at, :], low[at, :] = split(part[...])


def split_early(parts):
    rows, w = parts[0].shape
    return pl.pallas_call(
        split_kernel,
        out_shape=[jax.ShapeDtypeStruct((rows * len(parts), w), jnp.bfloat16)] * 2,
        compiler_params=pltpu.CompilerParams(vmem_limit_bytes=24 * MIB),
        cost_estimate=SHORT,
        name="split_early",
    )(*parts)


def gram_kernel(scale, n, ks, early_high, early_low, last, mine, theirs, high, low, packed):
    rows = last.shape[0]
    me = fibre_index()
    for i, k in enumerate(ks):
        at, piece = pl.ds(pl.multiple_of((me ^ k) * rows, rows), rows), slice(i * rows, (i + 1) * rows)
        high[at, :], low[at, :] = early_high[piece, :], early_low[piece, :]
    at = pl.ds(pl.multiple_of((me ^ (n - 2)) * rows, rows), rows)
    high[at, :], low[at, :] = split(last[...])
    m = high.shape[0]
    half = m // 2
    blocks = packed_blocks(m)
    for start in (0, half):
        rows, upto = slice(start, start + half), slice(0, start + half)
        g = dot3((high[rows, :], low[rows, :]), (high[upto, :], low[upto, :]), ((1,), (1,))) * scale
        for i, (r, c) in enumerate(blocks):
            if start <= r < start + half:
                packed[i * PART : (i + 1) * PART, :] = g[r - start : r - start + PART, c : c + LANES]
    me = fibre_index()
    piece = packed.shape[0] // n
    for k in range(0, n, 2):
        to = slice(k // 2 * piece, (k // 2 + 1) * piece)
        mine[to, :] = packed[pl.ds(pl.multiple_of(piece_of(me ^ k, n) * piece, SUB), piece), :]
        theirs[to, :] = packed[pl.ds(pl.multiple_of(piece_of(me ^ k ^ 1, n) * piece, SUB), piece), :]


def piece_of(device, n):
    return device


def gram_packed(parts, scale):
    rows, w = parts[0].shape
    n = len(parts)
    m = rows * n
    ks = [k for k in range(n) if k != n - 2]
    early = split_early([parts[k] for k in ks])
    last = after(parts[n - 2], *early)
    size = len(packed_blocks(m)) * PART
    half = jax.ShapeDtypeStruct((size // 2, LANES), jnp.float32)
    wide = jax.ShapeDtypeStruct((m, w), jnp.bfloat16)
    return pl.pallas_call(
        functools.partial(gram_kernel, scale, n, ks),
        out_shape=[half, half, wide, wide],
        scratch_shapes=[pltpu.VMEM((size, LANES), jnp.float32)],
        compiler_params=pltpu.CompilerParams(vmem_limit_bytes=24 * MIB),
        cost_estimate=SHORT,
        name="gram",
    )(*early, last)


def along_lanes(v, j):
    return jnp.broadcast_to(v[:, j : j + 1], (SUB, LANES))


def along_sublanes(ref, s):
    return jnp.broadcast_to(ref[s : s + 1, :], (SUB, LANES))


def factor_block(x, z, x_ref, z_ref, c_ref):
    sub = lax.broadcasted_iota(jnp.int32, (SUB, LANES), 0)
    eight = range(SUB)
    for g in range(len(x)):
        at = SUB * g
        x_ref[at : at + SUB, :], z_ref[at : at + SUB, :] = x[g], z[g]
        for t in eight:
            c_ref[SUB * (at + t) : SUB * (at + t + 1), :] = along_lanes(x[g], at + t)
        d = {(t, u): along_sublanes(c_ref, SUB * (at + u) + t) for u in eight for t in range(u + 1)}
        x_rows = [along_sublanes(x_ref, at + t) for t in eight]
        z_rows = [along_sublanes(z_ref, at + t) for t in eight]
        scale, r = [], {}
        for t in eight:
            scale.append(lax.rsqrt(d[t, t]))
            inverse = scale[t] * scale[t]
            x_rows[t], z_rows[t] = x_rows[t] * scale[t], z_rows[t] * scale[t]
            for u in range(t + 1, SUB):
                for v in range(t + 1, u + 1):
                    d[v, u] = d[v, u] - (d[t, v] * d[t, u]) * inverse
                r[t, u] = d[t, u] * scale[t]
                x_rows[u] = x_rows[u] - r[t, u] * x_rows[t]
                z_rows[u] = z_rows[u] - r[t, u] * z_rows[t]
        x[g], z[g] = x_rows[0], z_rows[0]
        for t in range(1, SUB):
            x[g], z[g] = jnp.where(sub == t, x_rows[t], x[g]), jnp.where(sub == t, z_rows[t], z[g])
        if g + 1 < len(x):
            cols = [along_lanes(x[g + 1], at + t) for t in eight]
            for t in eight:
                cols[t] = cols[t] * scale[t]
                for u in range(t + 1, SUB):
                    cols[u] = cols[u] - cols[t] * r[t, u]
                x[g + 1] = x[g + 1] - cols[t] * x_rows[t]
                z[g + 1] = z[g + 1] - cols[t] * z_rows[t]
        for t in reversed(eight):
            for u in range(t + 1, SUB):
                x_rows[t] = x_rows[t] - r[t, u] * x_rows[u]
                z_rows[t] = z_rows[t] - r[t, u] * z_rows[u]
            x_rows[t], z_rows[t] = x_rows[t] * scale[t], z_rows[t] * scale[t]
        for h in range(g + 2, len(x)):
            for t in eight:
                col = along_lanes(x[h], at + t)
                if t == 0:
                    x_sum, z_sum = col * x_rows[t], col * z_rows[t]
                else:
                    x_sum, z_sum = x_sum + col * x_rows[t], z_sum + col * z_rows[t]
            x[h], z[h] = x[h] - x_sum, z[h] - z_sum
    return jnp.concatenate(x, 0), jnp.concatenate(z, 0)


def factor_kernel(m, n, *refs):
    pieces, (l_ref, w_ref, a_ref, packed, *spare) = refs[:n], refs[n:]
    piece = pieces[0].shape[0]
    me = fibre_index()
    for k, part in enumerate(pieces):
        packed[pl.ds(pl.multiple_of(piece_of(me ^ k, n) * piece, SUB), piece), :] = part[...]
    for i, (r, c) in enumerate(packed_blocks(m)):
        a_ref[r : r + PART, c : c + LANES] = packed[i * PART : (i + 1) * PART, :]
    l_ref[...] = jnp.zeros((m, m), jnp.float32)
    w_ref[...] = jnp.zeros((m, m), jnp.float32)
    row = lax.broadcasted_iota(jnp.int32, (LANES, LANES), 0)
    lane = lax.broadcasted_iota(jnp.int32, (LANES, LANES), 1)
    groups = range(0, LANES, SUB)
    nt, nn = ((1,), (1,)), ((1,), (0,))
    for k in range(0, m, LANES):
        ks, before, rest = slice(k, k + LANES), slice(0, k), slice(k + LANES, m)
        block = a_ref[ks, ks]
        if k:
            block = block - dot_full(l_ref[ks, before], l_ref[ks, before], nt)
        below = a_ref[rest, ks] if k + LANES < m else None
        if k and below is not None:
            below = below - dot_full(l_ref[rest, before], l_ref[ks, before], nt)
        solved = dot_full(l_ref[ks, before], w_ref[before, before], nn) if k else None
        x = [block[s : s + SUB] for s in groups]
        z = [(lane[s : s + SUB] == row[s : s + SUB]).astype(jnp.float32) for s in groups]
        upper, inverse = factor_block(x, z, *spare)
        l_ref[ks, ks] = jnp.where(row >= lane, upper.T, 0.0)
        w_ref[ks, ks] = inverse
        if below is not None:
            l_ref[rest, ks] = dot_full(below, inverse, nt)
        if k:
            w_ref[ks, before] = -dot_full(inverse, solved, nn)


def factor_and_inverse(pieces, m):
    n = len(pieces)
    return pl.pallas_call(
        functools.partial(factor_kernel, m, n),
        out_shape=[jax.ShapeDtypeStruct((m, m), jnp.float32)] * 2,
        scratch_shapes=[
            pltpu.VMEM((m, m), jnp.float32),
            pltpu.VMEM((n * pieces[0].shape[0], LANES), jnp.float32),
            pltpu.VMEM((LANES, LANES), jnp.float32),
            pltpu.VMEM((LANES, LANES), jnp.float32),
            pltpu.VMEM((LANES * SUB, LANES), jnp.float32),
        ],
        compiler_params=pltpu.CompilerParams(vmem_limit_bytes=24 * MIB),
        cost_estimate=SHORT,
        name="factor",
    )(*pieces)


def rows_of(w_ref, wide, ks, rows):
    me = fibre_index()
    for i, k in enumerate(ks):
        piece = w_ref[pl.ds(pl.multiple_of((me ^ k) * rows, rows), rows), :]
        high, low = split(piece)
        for half, value in zip(wide, (high, low), strict=True):
            half[i * rows : (i + 1) * rows, :] = value


def send_kernel(ks, w_ref, high, low, *refs):
    outs, wide = refs[: len(ks)], refs[len(ks) :]
    rows, width = outs[0].shape
    rows_of(w_ref, wide, ks, rows)
    for start in range(0, width, width // 2):
        cols = slice(start, start + width // 2)
        solved = dot3((wide[0][...], wide[1][...]), (high[:, cols], low[:, cols]), ((1,), (0,)))
        for i, out in enumerate(outs):
            out[:, cols] = solved[i * rows : (i + 1) * rows]


def rows_to_send(w, high, low, ks, rows):
    m, width = high.shape
    return pl.pallas_call(
        functools.partial(send_kernel, ks),
        out_shape=[jax.ShapeDtypeStruct((rows, width), jnp.float32)] * len(ks),
        scratch_shapes=[pltpu.VMEM((len(ks) * rows, m), jnp.bfloat16)] * 2,
        compiler_params=pltpu.CompilerParams(vmem_limit_bytes=24 * MIB),
        cost_estimate=SHORT,
        name="send_rows",
    )(w, high, low)


def keep_kernel(n, w_ref, high, low, *refs):
    parts, outs, (twin_high, twin_low), wide = refs[:n], refs[n : n + 6], refs[n + 6 : n + 8], refs[n + 8 :]
    rows, width = outs[0].shape
    half = width // 2
    rows_of(w_ref, wide, (0, 1), rows)
    place_rows(parts, twin_high, twin_low)
    for (out, *near), h, l in ((outs[:3], high, low), (outs[3:], twin_high, twin_low)):
        for i in range(2):
            cols = slice(i * half, (i + 1) * half)
            solved = dot3((wide[0][...], wide[1][...]), (h[:, cols], l[:, cols]), ((1,), (0,)))
            out[:, cols] = solved[:rows]
            near[i][...] = solved[rows:]


def rows_to_keep(w, high, low, twin):
    m, width = high.shape
    n = len(twin)
    rows = m // n
    own = jax.ShapeDtypeStruct((rows, width), jnp.float32)
    near = jax.ShapeDtypeStruct((rows, width // 2), jnp.float32)
    return pl.pallas_call(
        functools.partial(keep_kernel, n),
        out_shape=[own, near, near, own, near, near],
        scratch_shapes=[pltpu.VMEM((m, width), jnp.bfloat16)] * 2 + [pltpu.VMEM((2 * rows, m), jnp.bfloat16)] * 2,
        compiler_params=pltpu.CompilerParams(vmem_limit_bytes=24 * MIB),
        cost_estimate=KEEP,
        name="keep_rows",
    )(w, high, low, *twin)


def permute(x, axis, bits):
    return lax.ppermute(x, axis, [(i, i ^ bits) for i in range(lax.axis_size(axis))])


def tree_sum(terms):
    while len(terms) > 1:
        terms = [a + b for a, b in zip(terms[::2], terms[1::2], strict=True)]
    return terms[0]


def after(x, *earlier):
    return lax.optimization_barrier((x, *earlier))[0]


def assemble_kernel(places, width, n_old, *refs):
    count = len(places)
    blocks, (out, sems) = refs[n_old : n_old + count], refs[n_old + count :]
    me = fibre_index()
    copies = []
    for i, ((k, start), block) in enumerate(zip(places, blocks, strict=True)):
        at = pl.multiple_of((me ^ k) * width, width) + start
        place = out.at[:, pl.ds(pl.multiple_of(at, LANES), block.shape[1])]
        copies.append(pltpu.make_async_copy(block, place, sems.at[i]))
    for copy in copies:
        copy.start()
    for copy in copies:
        copy.wait()


def assemble(blocks, rows, width, n, old=None):
    places = tuple(blocks)
    olds = () if old is None else (old,)
    return pl.pallas_call(
        functools.partial(assemble_kernel, places, width, len(olds)),
        out_shape=jax.ShapeDtypeStruct((rows, width * n), jnp.float32),
        in_specs=[pl.BlockSpec(memory_space=pl.ANY)] * (len(olds) + len(places)),
        out_specs=pl.BlockSpec(memory_space=pl.ANY),
        scratch_shapes=[pltpu.SemaphoreType.DMA((len(places),))],
        input_output_aliases={0: 0} if olds else {},
        compiler_params=pltpu.CompilerParams(vmem_limit_bytes=MIB),
        cost_estimate=SHORT,
        name="assemble",
    )(*olds, *blocks.values())


def local(tensor):
    n = lax.axis_size("fibre")
    groups = lax.axis_size("group")
    chips = n // 2
    me = lax.axis_index("fibre")
    rows, wide = tensor.shape
    m, width = rows * n, wide // n
    opposite = n - 2

    def block(x, j):
        return lax.dynamic_slice(x, (0, j * width), (rows, width))

    far = opposite + 1
    odd, even = list(range(3, n - 2, 2)), list(range(2, n - 2, 2))
    blocks = {far: block(tensor, me ^ far)}
    rest = after(tensor, blocks[far])
    blocks |= {k: block(rest, me ^ k) for k in range(far)}
    parts = [permute(blocks[k], "fibre", k) if k else blocks[0] for k in range(n)]
    twin = [block(rest, me ^ k ^ opposite) for k in range(opposite)] + [None, None]
    mine, theirs, high, low = gram_packed(parts, 1.0 / (width * n * groups))
    twin[1] = permute(after(twin[1], parts[far]), "fibre", 1)
    theirs, twin[1] = lax.optimization_barrier((theirs, twin[1]))
    mine = (mine + permute(theirs, "fibre", 1)).reshape(chips, -1, LANES)
    terms = [mine[k] if k == 0 else permute(mine[k], "fibre", 2 * k) for k in range(chips)]
    for k in even:
        twin[k] = permute(after(twin[k], terms[-1]), "fibre", k)
    piece = tree_sum(terms)
    piece = tree_sum([piece if k == 0 else permute(piece, "group", k) for k in range(groups)])
    piece, *arrived = lax.optimization_barrier((piece, *[twin[k] for k in even]))
    for k, x in zip(even, arrived, strict=True):
        twin[k] = x
    pieces = [None] * n
    for k in range(chips):
        pieces[2 * k] = piece if k == 0 else permute(piece, "fibre", 2 * k)
        pieces[2 * k + 1] = permute(pieces[2 * k], "fibre", 1)
    own = after(jnp.stack([blocks[0], blocks[1]]), *pieces[2::2])
    twin[opposite] = permute(own, "fibre", opposite)
    for k in odd:
        twin[k] = permute(after(twin[k], *pieces[3::2]), "fibre", k)
    factor, inverse = factor_and_inverse(pieces, m)
    ks = tuple(range(2, n - 2))
    solved = rows_to_send(inverse, high, low, ks, rows)
    sent = {k: permute(x, "fibre", k) for k, x in zip(ks, solved, strict=True)}
    twin[opposite] = after(twin[opposite], solved[0])
    twin[opposite + 1] = permute(twin[opposite][1], "fibre", 1)
    kept = rows_to_keep(inverse, high, low, twin)
    here = {(0, 0): kept[0], (opposite, 0): kept[3]}
    for k, near in ((1, kept[1:3]), (opposite + 1, kept[4:])):
        for i, x in enumerate(near):
            here[k, i * width // 2] = permute(x, "fibre", 1)
    basis = assemble(here | {(k, 0): sent[k] for k in even}, rows, width, n)
    if odd:
        basis = assemble({(k, 0): sent[k] for k in odd}, rows, width, n, basis)
    return (basis, factor)


def solution(mesh):
    return jax.shard_map(
        local,
        mesh=mesh,
        in_specs=(P("fibre", "group"),),
        out_specs=(P("fibre", "group"), P()),
        check_vma=False,
    )
```
